128 devices in a mesh: label: 32 (over y, x, z_hi), sub: 4 (over z_lo, core).
Axes of the slice: x: 4, y: 4, z: 4 (z_hi: 2, z_lo: 2; z = z_hi * 2 + z_lo), core: 2. Of those that a mesh axis runs over, the one named last changes fastest.
Arguments:
- features: bfloat16 [2048, 768], P(('label', 'sub')), may hold values from -6 to 6
- label_weight: bfloat16 [262144, 768], P(('label', 'sub')), may hold values from -0.21875 to 0.21875
- label_bias: float32 [262144], P(('label', 'sub')), may hold values from -5 to -1
- positive_ids: int32 [2048, 16], replicated, may hold values from 0 to 262143
- positive_counts: int32 [2048], replicated, may hold values from 1 to 16
Outputs:
- weight_grad: bfloat16 [262144, 768], P(('label', 'sub'))
- feature_grad: float32 [2048, 768], P(('label', 'sub'))
The draws below stay inside these ranges and needn't reach their ends.
Inputs may be any that keep to these rules, and one draw needn't show every extreme that they name: `positive_ids`: only the first positive_counts[q] entries of row q name positive labels; entries may repeat.
All inputs are finite; a program needn't handle non-finite values.
Results may differ from the reference program's by a relative error of at most 0.0075.
Values may be sent and summed in bfloat16 or wider, within the bound.
No kernel may reach another device: no remote copies, remote signals or barrier semaphores. Data moves between devices by JAX's collectives and lax.ppermute only.
A program may use at most 128 MiB of HBM per device.

```python
import jax
import jax.numpy as jnp
from jax import lax

D = 768
P_SIZE = 16
BLK = 512
LABELS = 262144
Q = 2048


def plant(result, own_key, least, largest):
    extent = result.shape
    place = [jax.random.randint(jax.random.fold_in(own_key, axis), (), 0, extent[axis]) for axis in range(len(extent))]
    result = result.at[tuple(place)].set(least)
    longest = extent.index(max(extent))
    place[longest] = (place[longest] + 1) % extent[longest]
    return result.at[tuple(place)].set(largest)


def level_of(stream_key, extent, shards, least, largest):
    def one(position, shards_of):
        draws = jax.random.uniform(jax.random.fold_in(jax.random.fold_in(stream_key, 6), position), (shards_of,), jnp.float32, least / len(shards), largest / len(shards))
        return jnp.repeat(jnp.exp(draws), extent[position] // shards_of).reshape((-1,) + (1,) * (len(extent) - position - 1))

    level = one(*shards[0])
    for cut in shards[1:]:
        level = level * one(*cut)
    return level


def centred(key, dims, width, bound, shards=(), kind=jnp.bfloat16):
    drawn = jax.random.normal(key, dims, jnp.float32) * width
    if len(shards) > 0:
        drawn = level_of(key, dims, shards, -0.22, 0.18) * drawn
    return jnp.clip(drawn, min=-bound, max=bound).astype(kind)


def setup_inputs(seed: int = 0) -> dict:
    streams_of = jax.random.split(jax.random.key(seed), 6)
    features = centred(streams_of[0], (Q, D), 1.0, 6.0, ((0, 128),))
    label_weight = centred(streams_of[1], (LABELS, D), D ** -0.5, 0.21875, ((0, 128),))
    label_bias = jnp.clip(-5.0 + 4.0 * jax.random.uniform(streams_of[2], (LABELS,), jnp.float32) ** level_of(streams_of[2], (LABELS,), ((0, 128),), -0.2, 0.2), -5.0, -1.0)
    positive_ids = plant(jax.random.randint(streams_of[3], (Q, P_SIZE), 0, LABELS), jax.random.fold_in(streams_of[3], 1), 0, LABELS - 1).astype(jnp.int32)
    positive_counts = plant(jax.random.randint(streams_of[4], (Q,), 1, P_SIZE + 1), jax.random.fold_in(streams_of[4], 1), 1, P_SIZE).astype(jnp.int32)
    return dict(features=features, label_weight=label_weight, label_bias=label_bias, positive_ids=positive_ids, positive_counts=positive_counts)


def reference(features, label_weight, label_bias, positive_ids, positive_counts):
    slots = jnp.arange(P_SIZE, dtype=jnp.int32)
    masked_ids = jnp.where(slots[None, :] < positive_counts[:, None], positive_ids, -1)
    nblocks = LABELS // BLK
    weight_blocks = label_weight.reshape(nblocks, BLK, D)
    bias_blocks = label_bias.reshape(nblocks, BLK)
    starts = jnp.arange(nblocks, dtype=jnp.int32) * BLK

    def step(accum, item):
        wblock, bblock, start = item
        logits = jnp.dot(features, wblock.T, preferred_element_type=jnp.float32) + bblock[None, :]
        labels_here = start + jnp.arange(BLK, dtype=jnp.int32)
        hits = jnp.any(masked_ids[:, :, None] == labels_here[None, None, :], axis=1)
        targets = hits.astype(jnp.float32)
        residual_grad = (jax.nn.sigmoid(logits) - targets).astype(jnp.bfloat16)
        wgrad = jnp.dot(residual_grad.T, features, preferred_element_type=jnp.float32).astype(jnp.bfloat16)
        accum = accum + jnp.dot(residual_grad, wblock, preferred_element_type=jnp.float32)
        return accum, wgrad

    init = jnp.zeros((Q, D), jnp.float32)
    feature_grad, wgrads = lax.scan(step, init, (weight_blocks, bias_blocks, starts))
    return wgrads.reshape(LABELS, D), feature_grad
```

```python
import functools

import jax
import jax.numpy as jnp
from jax import lax
from jax.experimental import pallas as pl
from jax.experimental.pallas import tpu as pltpu
from jax.sharding import PartitionSpec as P

AXES = ("label", "sub")
N = 4
STRIDE = {"y": 32, "x": 8, "z": 2}
LANES = 128
SUB = 1024
WSUB = 512
VMEM = pltpu.VMEM
WHOLE = pl.BlockSpec(memory_space=VMEM)


def vmem(x):
    return pltpu.with_memory_space_constraint(x, VMEM)


STAGES = {"first": ("z", "z"), "second": ("y", "x"), "third": ("x", "y")}


def shifted(stage, k):
    pairs = []
    for d in range(2 * N * N * N):
        step = STRIDE[STAGES[stage][d % 2]]
        at = d // step % N
        pairs.append((d, d + ((at + k) % N - at) * step))
    return pairs


def fetch(x, stage, k):
    return lax.ppermute(x, AXES, shifted(stage, -k))


def push(x, stage, k):
    return lax.ppermute(x, AXES, shifted(stage, k))


def swap(x):
    return lax.ppermute(x, AXES, [(d, d ^ 1) for d in range(2 * N * N * N)])


def words_kernel(rows, pos_ref, ids_ref, out_ref):
    core, base, own = pos_ref[0], pos_ref[1], pos_ref[2]
    pos3, pos2, pos1 = pos_ref[3], pos_ref[4], pos_ref[5]
    stride3 = jnp.where(core == 0, 8, 32)
    stride2 = jnp.where(core == 0, 32, 8)
    lane = lax.broadcasted_iota(jnp.int32, (rows, LANES), 1)

    def piece(p, carry):
        k, a, b = p // (N * N), p // N % N, p % N
        device = (pos3 + k) % N * stride3 + (pos2 + a) % N * stride2 + (pos1 + b) % N * 2 + core
        ids = ids_ref[pl.ds(pl.multiple_of(device * rows, rows), rows), :]
        rel = ids - base
        valid = jnp.logical_and(rel >= 0, rel < 2 * own)
        rel = jnp.where(valid, rel, 0) ^ (core * own)
        bit = jnp.where(valid, lax.shift_left(jnp.ones_like(rel), rel >> 7), 0)
        low = rel & (LANES - 1)
        words = jnp.zeros((rows, LANES), jnp.int32)
        for j in range(ids.shape[1]):
            words = words | jnp.where(lane == low[:, j : j + 1], bit[:, j : j + 1], 0)
        out_ref[pl.ds(pl.multiple_of(p * rows, rows), rows), :] = words
        return carry

    lax.fori_loop(0, N * N * N, piece, 0)


def label_words(pos, masked_ids, rows):
    return pl.pallas_call(
        functools.partial(words_kernel, rows),
        in_specs=[pl.BlockSpec(memory_space=pltpu.SMEM), WHOLE],
        out_specs=WHOLE,
        out_shape=VMEM((N * N * N * rows, LANES), jnp.int32),
        name="label_words",
        compiler_params=pltpu.CompilerParams(vmem_limit_bytes=8 << 20),
    )(pos, masked_ids)


def residual_kernel(chunk, f_ref, w0_ref, w1_ref, b0_ref, b1_ref, words_ref, r_ref, o_ref):
    f = f_ref[...]
    rows = f.shape[0]
    own = w0_ref.shape[0]
    words = words_ref[chunk * rows : (chunk + 1) * rows, :]
    for half, (w_ref, b_ref) in enumerate(((w0_ref, b0_ref), (w1_ref, b1_ref))):
        for s in range(0, own, SUB):
            logits = lax.dot_general(
                f, w_ref[s : s + SUB, :], (((1,), (1,)), ((), ())), preferred_element_type=jnp.float32
            )
            for g in range(0, SUB, LANES):
                at = half * own + s + g
                half_logits = logits[:, g : g + LANES] + b_ref[:, s + g : s + g + LANES]
                mark = jnp.int32(1 << (at // LANES) if at // LANES < 31 else -(1 << 31))
                offset = jnp.where((words & mark) != 0, -1.0, 1.0)
                r_ref[:, at : at + LANES] = (jnp.tanh(half_logits) + offset).astype(jnp.bfloat16)
    total = jnp.dot(r_ref[:, :own], w0_ref[...], preferred_element_type=jnp.float32)
    total = total + jnp.dot(r_ref[:, own:], w1_ref[...], preferred_element_type=jnp.float32)
    o_ref[...] = (total * 0.5).astype(o_ref.dtype)


def residual(chunk, f, w0, w1, b0, b1, words, out_type):
    rows, width = f.shape
    labels = 2 * w0.shape[0]
    return pl.pallas_call(
        functools.partial(residual_kernel, chunk),
        in_specs=[WHOLE] * 6,
        out_specs=[WHOLE, WHOLE],
        out_shape=[VMEM((rows, labels), jnp.bfloat16), VMEM((rows, width), out_type)],
        name="residual",
        cost_estimate=pl.CostEstimate(flops=4 * rows * labels * width, bytes_accessed=8 << 20, transcendentals=0),
        compiler_params=pltpu.CompilerParams(vmem_limit_bytes=12 << 20),
    )(vmem(f), vmem(w0), vmem(w1), vmem(b0), vmem(b1), vmem(words))


def weight_kernel(start, add, *refs):
    r_refs, f_refs, out_ref = refs[:N], refs[N : 2 * N], refs[-1]
    f = jnp.concatenate([ref[...] for ref in f_refs], axis=0)
    for s in range(0, out_ref.shape[0], WSUB):
        r = jnp.concatenate([ref[:, start + s : start + s + WSUB] for ref in r_refs], axis=0)
        total = lax.dot_general(r, f, (((0,), (0,)), ((), ())), preferred_element_type=jnp.float32)
        if add:
            total = total + refs[2 * N][s : s + WSUB, :].astype(jnp.float32)
        out_ref[s : s + WSUB, :] = total.astype(jnp.bfloat16)


def weight_product(rs, fs, start, count, other=None):
    rows, width = fs[0].shape
    extra = () if other is None else (vmem(other),)
    return pl.pallas_call(
        functools.partial(weight_kernel, start, other is not None),
        in_specs=[WHOLE] * (2 * N + len(extra)),
        out_specs=WHOLE,
        out_shape=VMEM((count, width), jnp.bfloat16),
        name="weight_product",
        cost_estimate=pl.CostEstimate(flops=2 * N * rows * count * width, bytes_accessed=4 << 20, transcendentals=0),
        compiler_params=pltpu.CompilerParams(vmem_limit_bytes=12 << 20),
    )(*[vmem(r) for r in rs], *[vmem(f) for f in fs], *extra)


def on_device(features, label_weight, label_bias, positive_ids, positive_counts):
    own, width = label_weight.shape
    rows = features.shape[0]
    me = lax.axis_index(AXES)
    core, z, x, y = me % 2, me // 2 % N, me // 8 % N, me // 32
    pos = jnp.stack([core, me // 2 * 2 * own, own, jnp.where(core == 0, x, y), jnp.where(core == 0, y, x), z])
    slots = jnp.arange(positive_ids.shape[1], dtype=jnp.int32)
    masked_ids = jnp.where(slots[None, :] < positive_counts[:, None], positive_ids, -1)

    f16 = features * jnp.bfloat16(0.5)
    f64 = jnp.concatenate([f16] + [fetch(f16, "first", k) for k in (1, 2, 3)], axis=0)
    f256 = jnp.concatenate([f64] + [fetch(f64, "second", k) for k in (1, 2, 3)], axis=0)
    fs = [f256] + [fetch(f256, "third", k) for k in (1, 2, 3)]

    b0 = (label_bias * 0.5).reshape(1, own)
    w0, w1, b1 = label_weight, swap(label_weight), swap(b0)
    words = label_words(pos, masked_ids, rows)

    rs, sums = [None] * N, None
    for k in (0, 1, 3, 2):
        rs[k], part = residual(k, fs[k], w0, w1, b0, b1, words, jnp.float32 if k == 0 else jnp.bfloat16)
        if k == 0:
            sums = part
        else:
            sums = sums + push(part, "third", k).astype(jnp.float32)

    half = own // 2
    others = [swap(weight_product(rs, fs, own + s, half)) for s in (0, half)]
    mine = [weight_product(rs, fs, s, half, other) for s, other in zip((0, half), others)]
    weight_grad = jnp.concatenate(mine, axis=0)

    for stage in ("second", "first"):
        count = sums.shape[0] // N
        sent = sums.astype(jnp.bfloat16)
        arrived = [push(sent[k * count : (k + 1) * count], stage, k) for k in (1, 2, 3)]
        sums = sums[:count]
        for part in arrived:
            sums = sums + part.astype(jnp.float32)
    return weight_grad, sums


def solution(mesh):
    split = P(AXES, None)
    return jax.shard_map(
        on_device,
        mesh=mesh,
        in_specs=(split, split, P(AXES), P(), P()),
        out_specs=(split, split),
        check_vma=False,
    )
```

```python
import functools

import jax
import jax.numpy as jnp
from jax import lax
from jax.experimental import pallas as pl
from jax.experimental.pallas import tpu as pltpu
from jax.sharding import PartitionSpec as P

AXES = ("label", "sub")
N = 4
STRIDE = {"y": 32, "x": 8, "z": 2}
LANES = 128
SUB = 1024
WSUB = 512
VMEM = pltpu.VMEM
WHOLE = pl.BlockSpec(memory_space=VMEM)
SCALARS = pl.BlockSpec(memory_space=pltpu.SMEM)
ORDER = pl.BlockSpec(memory_space=pl.ANY)
STAYS = pl.BlockSpec(memory_space=pltpu.HBM)


def vmem(x):
    return pltpu.with_memory_space_constraint(x, VMEM)


def hbm(x):
    return pltpu.with_memory_space_constraint(x, pltpu.HBM)


def params(mebibytes):
    return pltpu.CompilerParams(vmem_limit_bytes=mebibytes << 20)


def cost(flops):
    return pl.CostEstimate(flops=flops // 8, bytes_accessed=0, transcendentals=0)


STAGES = {"first": ("z", "z"), "second": ("y", "x"), "third": ("x", "y")}


def shifted(stage, k):
    pairs = []
    for d in range(2 * N * N * N):
        step = STRIDE[STAGES[stage][d % 2]]
        at = d // step % N
        pairs.append((d, d + ((at + k) % N - at) * step))
    return pairs


def fetch(x, stage, k):
    return lax.ppermute(x, AXES, shifted(stage, -k))


def push(x, stage, k):
    return lax.ppermute(x, AXES, shifted(stage, k))


def swap(x):
    return lax.ppermute(x, AXES, [(d, d ^ 1) for d in range(2 * N * N * N)])


def prepare_kernel(piece, pos_ref, b1_ref, w_ref, ids_hbm, counts_hbm, b0_hbm, *refs):
    w_out, words_out, half_out, ids_ref, counts_ref, b0_ref, sems = refs[-7:]
    pairs = ((ids_hbm, ids_ref), (counts_hbm, counts_ref), (b0_hbm, b0_ref), (w_ref, w_out))
    copies = [pltpu.make_async_copy(src, dst, sems.at[i]) for i, (src, dst) in enumerate(pairs)]
    for copy in copies:
        copy.start()
    copies[0].wait()
    copies[1].wait()
    core, base, own = pos_ref[0], pos_ref[1], pos_ref[2]
    slots, queries = ids_ref.shape
    row = lax.broadcasted_iota(jnp.int32, (8, LANES), 0)
    slot = lax.broadcasted_iota(jnp.int32, (slots, LANES), 0)
    lane = lax.broadcasted_iota(jnp.int32, (slots, LANES), 1)
    kept = (lane // piece) % 2 == core
    shift = jnp.where(core == 0, piece, LANES - piece)

    def packed(ref, q):
        other = pltpu.roll(jnp.broadcast_to(ref[:, q + LANES : q + 2 * LANES], (slots, LANES)), shift, 1)
        return jnp.where(kept, jnp.broadcast_to(ref[:, q : q + LANES], (slots, LANES)), other)

    for q in range(0, queries, 2 * LANES):
        rel = packed(ids_ref, q) - base
        valid = jnp.logical_and(rel >= 0, rel < 2 * own)
        valid = jnp.logical_and(valid, slot < packed(counts_ref, q))
        rel = jnp.where(valid, rel, 0) ^ (core * own)
        bit = jnp.where(valid, lax.shift_left(jnp.ones_like(rel), rel >> 7), 0)
        low = rel & (LANES - 1)
        parts = []
        for g in range(0, LANES, 8):
            word = jnp.zeros((8, LANES), jnp.int32)
            for j in range(slots):
                word = word | jnp.where(low[j : j + 1, :] == row + g, bit[j : j + 1, :], 0)
            parts.append(word)
        words_out[q // 2 : q // 2 + LANES, :] = jnp.concatenate(parts, axis=0).T
    copies[2].wait()
    half_out[...] = 0.5 * jnp.concatenate([b0_ref[...], b1_ref[...]], axis=1)
    copies[3].wait()


def prepare(piece, pos, w, ids, counts, b0, b1, after=()):
    return pl.pallas_call(
        functools.partial(prepare_kernel, piece),
        in_specs=[SCALARS, WHOLE] + [STAYS] * 4 + [ORDER] * len(after),
        out_specs=[WHOLE] * 3,
        out_shape=[
            VMEM(w.shape, w.dtype),
            VMEM((ids.shape[1] // 2, LANES), jnp.int32),
            VMEM((1, 2 * b0.shape[1]), jnp.float32),
        ],
        scratch_shapes=[
            VMEM(ids.shape, ids.dtype),
            VMEM(counts.shape, counts.dtype),
            VMEM(b0.shape, b0.dtype),
            pltpu.SemaphoreType.DMA((4,)),
        ],
        name="prepare",
        cost_estimate=cost(0),
        compiler_params=params(8),
    )(pos, b1, *[hbm(x) for x in (w, ids, counts, b0)], *after)


def load_kernel(x_ref, *refs):
    refs[-1][...] = x_ref[...]


def load(x, after):
    return pl.pallas_call(
        load_kernel,
        in_specs=[WHOLE] + [ORDER] * len(after),
        out_specs=WHOLE,
        out_shape=VMEM(x.shape, x.dtype),
        name="load",
        cost_estimate=cost(0),
        compiler_params=params(4),
    )(hbm(x), *after)


def join_kernel(count, factor, *refs):
    refs[-1][...] = jnp.concatenate([ref[...] for ref in refs[:count]], axis=0) * jnp.bfloat16(factor)


def join(parts, factor=1.0, after=()):
    rows, width = parts[0].shape
    return pl.pallas_call(
        functools.partial(join_kernel, len(parts), factor),
        in_specs=[WHOLE] * len(parts) + [ORDER] * len(after),
        out_specs=WHOLE,
        out_shape=VMEM((len(parts) * rows, width), parts[0].dtype),
        name="join",
        cost_estimate=cost(0),
        compiler_params=params(4),
    )(*[vmem(x) for x in parts], *after)


def residual_kernel(chunk, piece, again, pos_ref, f_ref, w0_ref, w1_ref, b_ref, words_ref, *refs):
    r_ref, o_ref = refs[-3:-1] if again else refs[-2:]
    f = f_ref[...]
    if again:
        refs[-1][...] = f
    own = w0_ref.shape[0]
    core, third, second, first = pos_ref[0], pos_ref[3], pos_ref[4], pos_ref[5]
    stride3 = jnp.where(core == 0, STRIDE["x"], STRIDE["y"]) // 2
    stride2 = jnp.where(core == 0, STRIDE["y"], STRIDE["x"]) // 2
    words = []
    for a in range(N):
        for b in range(N):
            chip = (third + chunk) % N * stride3 + (second + a) % N * stride2 + (first + b) % N
            near = chip % 8 < 4
            place = chip // 8 * 8 + chip % 4 * 2 + jnp.where(near, core, 1 - core)
            words.append(words_ref[pl.ds(pl.multiple_of(place * piece, piece), piece), :])
    words = jnp.concatenate(words, axis=0)
    for half, w_ref in enumerate((w0_ref, w1_ref)):
        for s in range(0, own, SUB):
            logits = lax.dot_general(
                f, w_ref[s : s + SUB, :], (((1,), (1,)), ((), ())), preferred_element_type=jnp.float32
            )
            for g in range(0, SUB, LANES):
                at = half * own + s + g
                half_logits = logits[:, g : g + LANES] + b_ref[:, at : at + LANES]
                mark = jnp.int32(1 << (at // LANES) if at // LANES < 31 else -(1 << 31))
                offset = jnp.where((words & mark) != 0, -1.0, 1.0)
                r_ref[:, at : at + LANES] = (jnp.tanh(half_logits) + offset).astype(jnp.bfloat16)
    w = jnp.concatenate([w0_ref[...], w1_ref[...]], axis=0)
    total = jnp.dot(r_ref[...], w, preferred_element_type=jnp.float32)
    o_ref[...] = (total * 0.5).astype(o_ref.dtype)


def residual(chunk, piece, pos, f, w0, w1, b, words, out_type, after=(), again=False):
    rows, width = f.shape
    labels = 2 * w0.shape[0]
    return pl.pallas_call(
        functools.partial(residual_kernel, chunk, piece, again),
        in_specs=[SCALARS] + [WHOLE] * 5 + [ORDER] * len(after),
        out_specs=[WHOLE] * (3 if again else 2),
        out_shape=[VMEM((rows, labels), jnp.bfloat16), VMEM((rows, width), out_type)] + [VMEM(f.shape, f.dtype)] * again,
        name="residual",
        cost_estimate=cost(4 * rows * labels),
        compiler_params=params(12),
    )(pos, *[vmem(x) for x in (f, w0, w1, b, words)], *after)


def weight_partial_kernel(start, *refs):
    r_refs, f_refs, out_ref = refs[:N], refs[N : 2 * N], refs[-1]
    f = jnp.concatenate([ref[...] for ref in f_refs], axis=0)
    for s in range(0, out_ref.shape[0], WSUB):
        r = jnp.concatenate([ref[:, start + s : start + s + WSUB] for ref in r_refs], axis=0)
        total = lax.dot_general(r, f, (((0,), (0,)), ((), ())), preferred_element_type=jnp.float32)
        out_ref[s : s + WSUB, :] = total.astype(jnp.bfloat16)


def weight_partial(rs, fs, start, count, after):
    rows, width = fs[0].shape
    return pl.pallas_call(
        functools.partial(weight_partial_kernel, start),
        in_specs=[WHOLE] * (2 * N) + [ORDER] * len(after),
        out_specs=WHOLE,
        out_shape=VMEM((count, width), jnp.bfloat16),
        name="weight_partial",
        cost_estimate=cost(2 * rows * count),
        compiler_params=params(12),
    )(*[vmem(x) for x in rs], *[vmem(x) for x in fs], *after)


def weight_rows_kernel(start, *refs):
    r_refs, f_refs, other_ref = refs[:N], refs[N : 2 * N], refs[2 * N]
    out_ref, done_ref, rows_ref, sems = refs[-4:]
    f = jnp.concatenate([ref[...] for ref in f_refs], axis=0)
    copies = []
    for s in range(0, rows_ref.shape[0], WSUB):
        r = jnp.concatenate([ref[:, start + s : start + s + WSUB] for ref in r_refs], axis=0)
        total = lax.dot_general(r, f, (((0,), (0,)), ((), ())), preferred_element_type=jnp.float32)
        total = total + other_ref[s : s + WSUB, :].astype(jnp.float32)
        rows_ref[s : s + WSUB, :] = total.astype(jnp.bfloat16)
        copy = pltpu.make_async_copy(
            rows_ref.at[pl.ds(s, WSUB)], out_ref.at[pl.ds(start + s, WSUB)], sems.at[s // WSUB]
        )
        copy.start()
        copies.append(copy)
    done_ref[...] = jnp.zeros_like(done_ref)
    for copy in copies:
        copy.wait()


def weight_rows(rs, fs, start, count, own, other, whole, after):
    rows, width = fs[0].shape
    extra, aliases = tuple(after), {}
    if whole is not None:
        extra, aliases = (whole,) + extra, {2 * N + 1: 0}
    return pl.pallas_call(
        functools.partial(weight_rows_kernel, start),
        in_specs=[WHOLE] * (2 * N + 1) + [ORDER] * len(extra),
        out_specs=[ORDER, WHOLE],
        out_shape=[jax.ShapeDtypeStruct((own, width), jnp.bfloat16), VMEM((8, LANES), jnp.float32)],
        scratch_shapes=[VMEM((count, width), jnp.bfloat16), pltpu.SemaphoreType.DMA((count // WSUB,))],
        input_output_aliases=aliases,
        name="weight_rows",
        cost_estimate=cost(16 * N * rows * count * width),
        compiler_params=params(12),
    )(*[vmem(x) for x in rs], *[vmem(x) for x in fs], vmem(other), *extra)


def add_kernel(count, own_ref, a_ref, b_ref, c_ref, *refs):
    rows = a_ref.shape[0]
    total = own_ref[:rows, :] + a_ref[...].astype(jnp.float32)
    total = total + b_ref[...].astype(jnp.float32) + c_ref[...].astype(jnp.float32)
    outs = refs[len(refs) - count :]
    step = rows // count
    outs[0][...] = total[:step, :]
    for k in range(1, count):
        outs[k][...] = total[k * step : (k + 1) * step, :].astype(jnp.bfloat16)


def add(own, parts, count, after=()):
    rows, width = parts[0].shape
    kinds = [jnp.float32] + [jnp.bfloat16] * (count - 1)
    return pl.pallas_call(
        functools.partial(add_kernel, count),
        in_specs=[WHOLE] * 4 + [ORDER] * len(after),
        out_specs=[WHOLE] * count,
        out_shape=[VMEM((rows // count, width), kind) for kind in kinds],
        name="add",
        cost_estimate=cost(3 * 10**11),
        compiler_params=params(4),
    )(vmem(own), *[vmem(x) for x in parts], *after)


def on_device(features, label_weight, label_bias, positive_ids, positive_counts):
    own, width = label_weight.shape
    piece = features.shape[0]
    me = lax.axis_index(AXES)
    core, z, x, y = me % 2, me // 2 % N, me // 8 % N, me // 32
    pos = jnp.stack([core, me // 2 * 2 * own, own, jnp.where(core == 0, x, y), jnp.where(core == 0, y, x), z])

    b0 = label_bias.reshape(1, own)
    w1, b1 = swap(label_weight), swap(b0)
    f64 = join([load(features, (b1,))] + [fetch(features, "first", k) for k in (1, 2, 3)], factor=0.5)
    w0, words, b = prepare(piece, pos, label_weight, positive_ids.T, positive_counts.reshape(1, -1), b0, b1, after=(f64,))
    f256 = join([f64] + [fetch(f64, "second", k) for k in (1, 2, 3)], after=(words,))
    fs = [f256, fetch(f256, "third", 1), None, fetch(f256, "third", 3)]

    rs = [None] * N
    rs[0], sums, again = residual(0, piece, pos, f256, w0, w1, b, words, jnp.float32, again=True)
    fs[2] = fetch(again, "third", 2)
    arrived, after = [], (sums,)
    for k in (1, 3, 2):
        rs[k], part = residual(k, piece, pos, fs[k], w0, w1, b, words, jnp.bfloat16, after)
        after = (part,)
        arrived.append(push(part, "third", k))

    half = own // 2
    theirs = [swap(weight_partial(rs, fs, own + s, half, x)) for s, x in zip((0, half), ((), arrived[:2]))]
    sums, *sent = add(sums, arrived, N)
    arrived = [push(x, "second", k) for k, x in zip((1, 2, 3), sent)]
    weight_grad, done = weight_rows(rs, fs, 0, half, own, theirs[0], None, sent)
    sums, *sent = add(sums, arrived, N, after=(done,))
    arrived = [push(x, "first", k) for k, x in zip((1, 2, 3), sent)]
    weight_grad, _ = weight_rows(rs, fs, half, half, own, theirs[1], weight_grad, sent)
    for x in arrived:
        sums = sums + x.astype(jnp.float32)
    return weight_grad, sums


def solution(mesh):
    split = P(AXES, None)
    return jax.shard_map(
        on_device,
        mesh=mesh,
        in_specs=(split, split, P(AXES), P(), P()),
        out_specs=(split, split),
        check_vma=False,
    )
```

```python
import functools

import jax
import jax.numpy as jnp
from jax import lax
from jax.experimental import pallas as pl
from jax.experimental.pallas import tpu as pltpu
from jax.sharding import PartitionSpec as P

AXES = ("label", "sub")
N = 4
STRIDE = {"y": 32, "x": 8, "z": 2}
LANES = 128
SUB = 1024
WSUB = 512
FSUB = 256
VMEM = pltpu.VMEM
WHOLE = pl.BlockSpec(memory_space=VMEM)
SCALARS = pl.BlockSpec(memory_space=pltpu.SMEM)
ORDER = pl.BlockSpec(memory_space=pl.ANY)
STAYS = pl.BlockSpec(memory_space=pltpu.HBM)


def vmem(x):
    return pltpu.with_memory_space_constraint(x, VMEM)


def hbm(x):
    return pltpu.with_memory_space_constraint(x, pltpu.HBM)


def params(mebibytes):
    return pltpu.CompilerParams(vmem_limit_bytes=mebibytes << 20)


def cost(flops):
    return pl.CostEstimate(flops=flops // 8, bytes_accessed=0, transcendentals=0)


STAGES = {"first": ("z", "z"), "second": ("y", "x"), "third": ("x", "y")}


def shifted(stage, k):
    pairs = []
    for d in range(2 * N * N * N):
        step = STRIDE[STAGES[stage][d % 2]]
        at = d // step % N
        pairs.append((d, d + ((at + k) % N - at) * step))
    return pairs


def fetch(x, stage, k):
    return lax.ppermute(x, AXES, shifted(stage, -k))


def push(x, stage, k):
    return lax.ppermute(x, AXES, shifted(stage, k))


def swap(x):
    return lax.ppermute(x, AXES, [(d, d ^ 1) for d in range(2 * N * N * N)])


def prepare_kernel(piece, pos_ref, b1_ref, w_ref, ids_hbm, counts_hbm, b0_hbm, *refs):
    w_out, words_out, half_out, ids_ref, counts_ref, b0_ref, sems = refs[-7:]
    pairs = ((ids_hbm, ids_ref), (counts_hbm, counts_ref), (b0_hbm, b0_ref), (w_ref, w_out))
    copies = [pltpu.make_async_copy(src, dst, sems.at[i]) for i, (src, dst) in enumerate(pairs)]
    for copy in copies:
        copy.start()
    copies[0].wait()
    copies[1].wait()
    core, base, own = pos_ref[0], pos_ref[1], pos_ref[2]
    slots, queries = ids_ref.shape
    row = lax.broadcasted_iota(jnp.int32, (8, LANES), 0)
    slot = lax.broadcasted_iota(jnp.int32, (slots, LANES), 0)
    third, second, first = pos_ref[3], pos_ref[4], pos_ref[5]
    lane = lax.broadcasted_iota(jnp.int32, (slots, LANES), 1)
    kept = (lane // piece) % 2 == core
    shift = jnp.where(core == 0, piece, LANES - piece)

    def packed(ref, q):
        other = pltpu.roll(jnp.broadcast_to(ref[:, q + LANES : q + 2 * LANES], (slots, LANES)), shift, 1)
        return jnp.where(kept, jnp.broadcast_to(ref[:, q : q + LANES], (slots, LANES)), other)

    for q in range(0, queries, 2 * LANES):
        rel = packed(ids_ref, q) - base
        valid = jnp.logical_and(rel >= 0, rel < 2 * own)
        valid = jnp.logical_and(valid, slot < packed(counts_ref, q))
        rel = jnp.where(valid, rel, 0) ^ (core * own)
        bit = jnp.where(valid, lax.shift_left(jnp.ones_like(rel), rel >> 7), 0)
        low = rel & (LANES - 1)
        parts = []
        for g in range(0, LANES, 8):
            word = jnp.zeros((8, LANES), jnp.int32)
            for j in range(slots):
                word = word | jnp.where(low[j : j + 1, :] == row + g, bit[j : j + 1, :], 0)
            parts.append(word)
        words = jnp.concatenate(parts, axis=0).T
        for place in range(LANES // piece):
            near = place % 2 == core
            chip = q // (2 * piece) + place // 2 + jnp.where(near, 0, N)
            y, x, z = chip // (N * N), chip // N % N, chip % N
            at3 = (jnp.where(core == 0, x, y) - third + N) % N
            at2 = (jnp.where(core == 0, y, x) - second + N) % N
            row_at = ((at3 * N + at2) * N + (z - first + N) % N) * piece
            words_out[pl.ds(pl.multiple_of(row_at, piece), piece), :] = words[place * piece : (place + 1) * piece, :]
    copies[2].wait()
    half_out[...] = 0.5 * jnp.concatenate([b0_ref[...], b1_ref[...]], axis=1)
    copies[3].wait()


def prepare(piece, pos, w, ids, counts, b0, b1, after=()):
    return pl.pallas_call(
        functools.partial(prepare_kernel, piece),
        in_specs=[SCALARS, WHOLE] + [STAYS] * 4 + [ORDER] * len(after),
        out_specs=[WHOLE] * 3,
        out_shape=[
            VMEM(w.shape, w.dtype),
            VMEM((ids.shape[1] // 2, LANES), jnp.int32),
            VMEM((1, 2 * b0.shape[1]), jnp.float32),
        ],
        scratch_shapes=[
            VMEM(ids.shape, ids.dtype),
            VMEM(counts.shape, counts.dtype),
            VMEM(b0.shape, b0.dtype),
            pltpu.SemaphoreType.DMA((4,)),
        ],
        name="prepare",
        cost_estimate=cost(0),
        compiler_params=params(8),
    )(pos, b1, *[hbm(x) for x in (w, ids, counts, b0)], *after)


def load_kernel(x_ref, *refs):
    refs[-1][...] = x_ref[...]


def load(x, after):
    return pl.pallas_call(
        load_kernel,
        in_specs=[WHOLE] + [ORDER] * len(after),
        out_specs=WHOLE,
        out_shape=VMEM(x.shape, x.dtype),
        name="load",
        cost_estimate=cost(0),
        compiler_params=params(4),
    )(hbm(x), *after)


def join_kernel(count, factor, *refs):
    refs[-1][...] = jnp.concatenate([ref[...] for ref in refs[:count]], axis=0) * jnp.bfloat16(factor)


def join(parts, factor=1.0, after=()):
    rows, width = parts[0].shape
    return pl.pallas_call(
        functools.partial(join_kernel, len(parts), factor),
        in_specs=[WHOLE] * len(parts) + [ORDER] * len(after),
        out_specs=WHOLE,
        out_shape=VMEM((len(parts) * rows, width), parts[0].dtype),
        name="join",
        cost_estimate=cost(0),
        compiler_params=params(4),
    )(*[vmem(x) for x in parts], *after)


def residual_kernel(chunk, again, f_ref, w0_ref, w1_ref, b_ref, words_ref, *refs):
    r_ref, o_ref = refs[-3:-1] if again else refs[-2:]
    f = f_ref[...]
    if again:
        refs[-1][...] = f
    rows, own = f.shape[0], w0_ref.shape[0]
    words = words_ref[chunk * rows : (chunk + 1) * rows, :]
    for half, w_ref in enumerate((w0_ref, w1_ref)):
        for s in range(0, own, SUB):
            logits = lax.dot_general(
                f, w_ref[s : s + SUB, :], (((1,), (1,)), ((), ())), preferred_element_type=jnp.float32
            )
            for g in range(0, SUB, LANES):
                at = half * own + s + g
                half_logits = logits[:, g : g + LANES] + b_ref[:, at : at + LANES]
                mark = jnp.int32(1 << (at // LANES) if at // LANES < 31 else -(1 << 31))
                offset = jnp.where((words & mark) != 0, -1.0, 1.0)
                r_ref[:, at : at + LANES] = (jnp.tanh(half_logits) + offset).astype(jnp.bfloat16)
    w = jnp.concatenate([w0_ref[...], w1_ref[...]], axis=0)
    total = jnp.dot(r_ref[...], w, preferred_element_type=jnp.float32)
    o_ref[...] = (total * 0.5).astype(o_ref.dtype)


def residual(chunk, f, w0, w1, b, words, out_type, after=(), again=False):
    rows, width = f.shape
    labels = 2 * w0.shape[0]
    return pl.pallas_call(
        functools.partial(residual_kernel, chunk, again),
        in_specs=[WHOLE] * 5 + [ORDER] * len(after),
        out_specs=[WHOLE] * (3 if again else 2),
        out_shape=[VMEM((rows, labels), jnp.bfloat16), VMEM((rows, width), out_type)] + [VMEM(f.shape, f.dtype)] * again,
        name="residual",
        cost_estimate=cost(4 * rows * labels),
        compiler_params=params(12),
    )(*[vmem(x) for x in (f, w0, w1, b, words)], *after)


def weight_partial_kernel(start, *refs):
    r_refs, f_refs, out_ref = refs[:N], refs[N : 2 * N], refs[-1]
    f = jnp.concatenate([ref[...] for ref in f_refs], axis=0)
    for s in range(0, out_ref.shape[0], WSUB):
        r = jnp.concatenate([ref[:, start + s : start + s + WSUB] for ref in r_refs], axis=0)
        total = lax.dot_general(r, f, (((0,), (0,)), ((), ())), preferred_element_type=jnp.float32)
        out_ref[s : s + WSUB, :] = total.astype(out_ref.dtype)


def weight_partial(rs, fs, start, count, kind, after=()):
    rows, width = fs[0].shape
    return pl.pallas_call(
        functools.partial(weight_partial_kernel, start),
        in_specs=[WHOLE] * (2 * N) + [ORDER] * len(after),
        out_specs=WHOLE,
        out_shape=VMEM((count, width), kind),
        name="weight_partial",
        cost_estimate=cost(2 * rows * count),
        compiler_params=params(12),
    )(*[vmem(x) for x in rs], *[vmem(x) for x in fs], *after)


def weight_rows_kernel(start, *refs):
    r_refs, f_refs, other_ref = refs[:N], refs[N : 2 * N], refs[2 * N]
    out_ref, done_ref, rows_ref, sems = refs[-4:]
    f = jnp.concatenate([ref[...] for ref in f_refs], axis=0)
    copies = []
    for s in range(0, rows_ref.shape[0], WSUB):
        r = jnp.concatenate([ref[:, start + s : start + s + WSUB] for ref in r_refs], axis=0)
        total = lax.dot_general(r, f, (((0,), (0,)), ((), ())), preferred_element_type=jnp.float32)
        total = total + other_ref[s : s + WSUB, :].astype(jnp.float32)
        rows_ref[s : s + WSUB, :] = total.astype(jnp.bfloat16)
        copy = pltpu.make_async_copy(
            rows_ref.at[pl.ds(s, WSUB)], out_ref.at[pl.ds(start + s, WSUB)], sems.at[s // WSUB]
        )
        copy.start()
        copies.append(copy)
    done_ref[...] = jnp.zeros_like(done_ref)
    for copy in copies:
        copy.wait()


def weight_rows(rs, fs, start, count, own, other, after):
    rows, width = fs[0].shape
    return pl.pallas_call(
        functools.partial(weight_rows_kernel, start),
        in_specs=[WHOLE] * (2 * N + 1) + [ORDER] * len(after),
        out_specs=[ORDER, WHOLE],
        out_shape=[jax.ShapeDtypeStruct((own, width), jnp.bfloat16), VMEM((8, LANES), jnp.float32)],
        scratch_shapes=[VMEM((count, width), jnp.bfloat16), pltpu.SemaphoreType.DMA((count // WSUB,))],
        name="weight_rows",
        cost_estimate=cost(16 * N * rows * count * width),
        compiler_params=params(12),
    )(*[vmem(x) for x in rs], *[vmem(x) for x in fs], vmem(other), *after)


def finish_kernel(start, mine_ref, other_ref, *refs):
    out_ref, done_ref, rows_ref, sems = refs[-4:]
    done_ref[...] = jnp.zeros_like(done_ref)
    copies = []
    for i, s in enumerate(range(0, rows_ref.shape[0], FSUB)):
        total = mine_ref[s : s + FSUB, :] + other_ref[s : s + FSUB, :].astype(jnp.float32)
        rows_ref[s : s + FSUB, :] = total.astype(jnp.bfloat16)
        copies.append(
            pltpu.make_async_copy(rows_ref.at[pl.ds(s, FSUB)], out_ref.at[pl.ds(start + s, FSUB)], sems.at[i])
        )
        copies[-1].start()
    for copy in copies:
        copy.wait()


def finish_rows(mine, other, whole, start, after):
    count, width = mine.shape
    return pl.pallas_call(
        functools.partial(finish_kernel, start),
        in_specs=[WHOLE] * 2 + [ORDER] * (1 + len(after)),
        out_specs=[ORDER, WHOLE],
        out_shape=[jax.ShapeDtypeStruct(whole.shape, whole.dtype), VMEM((8, LANES), jnp.float32)],
        scratch_shapes=[VMEM((count, width), jnp.bfloat16), pltpu.SemaphoreType.DMA((count // FSUB,))],
        input_output_aliases={2: 0},
        name="finish_rows",
        cost_estimate=cost(16 * N * count * count * width // 4),
        compiler_params=params(8),
    )(vmem(mine), vmem(other), whole, *after)


def add_kernel(count, own_ref, a_ref, b_ref, c_ref, *refs):
    rows = a_ref.shape[0]
    total = own_ref[:rows, :] + a_ref[...].astype(jnp.float32)
    total = total + b_ref[...].astype(jnp.float32) + c_ref[...].astype(jnp.float32)
    outs = refs[len(refs) - count :]
    step = rows // count
    outs[0][...] = total[:step, :]
    for k in range(1, count):
        outs[k][...] = total[k * step : (k + 1) * step, :].astype(jnp.bfloat16)


def add(own, parts, count, after=()):
    rows, width = parts[0].shape
    kinds = [jnp.float32] + [jnp.bfloat16] * (count - 1)
    return pl.pallas_call(
        functools.partial(add_kernel, count),
        in_specs=[WHOLE] * 4 + [ORDER] * len(after),
        out_specs=[WHOLE] * count,
        out_shape=[(VMEM if count > 1 else jax.ShapeDtypeStruct)((rows // count, width), kind) for kind in kinds],
        name="add",
        cost_estimate=cost(3 * 10**11),
        compiler_params=params(4),
    )(vmem(own), *[vmem(x) for x in parts], *after)


def on_device(features, label_weight, label_bias, positive_ids, positive_counts):
    own, width = label_weight.shape
    piece = features.shape[0]
    me = lax.axis_index(AXES)
    core, z, x, y = me % 2, me // 2 % N, me // 8 % N, me // 32
    pos = jnp.stack([core, me // 2 * 2 * own, own, jnp.where(core == 0, x, y), jnp.where(core == 0, y, x), z])

    b0 = label_bias.reshape(1, own)
    w1, b1 = swap(label_weight), swap(b0)
    f64 = join([load(features, (b1,))] + [fetch(features, "first", k) for k in (1, 2, 3)], factor=0.5)
    w0, words, b = prepare(piece, pos, label_weight, positive_ids.T, positive_counts.reshape(1, -1), b0, b1, after=(f64,))
    f256 = join([f64] + [fetch(f64, "second", k) for k in (1, 2, 3)], after=(words,))
    fs = [f256, fetch(f256, "third", 1), None, fetch(f256, "third", 3)]

    rs = [None] * N
    rs[0], sums, again = residual(0, f256, w0, w1, b, words, jnp.float32, again=True)
    fs[2] = fetch(again, "third", 2)
    arrived, after = [], (sums,)
    for k in (1, 3, 2):
        rs[k], part = residual(k, fs[k], w0, w1, b, words, jnp.bfloat16, after)
        after = (part,)
        arrived.append(push(part, "third", k))

    half = own // 2
    partial = functools.partial(weight_partial, rs, fs)
    theirs = [partial(own, half, jnp.bfloat16, arrived[:1]), partial(own + half, half, jnp.bfloat16, arrived[1:2])]
    mine = partial(half, half, jnp.float32, theirs)
    theirs = [swap(x) for x in theirs]
    sums, *sent = add(sums, arrived, N, after=(mine,))
    arrived = [push(x, "second", k) for k, x in zip((1, 2, 3), sent)]
    weight_grad, done = weight_rows(rs, fs, 0, half, own, theirs[0], sent)
    sums, *sent = add(sums, arrived, N, after=(done,))
    arrived = [push(x, "first", k) for k, x in zip((1, 2, 3), sent)]
    weight_grad, done = finish_rows(mine, theirs[1], weight_grad, half, sent)
    (sums,) = add(sums, arrived, 1, after=(done,))
    return weight_grad, sums


def solution(mesh):
    split = P(AXES, None)
    return jax.shard_map(
        on_device,
        mesh=mesh,
        in_specs=(split, split, P(AXES), P(), P()),
        out_specs=(split, split),
        check_vma=False,
    )
```

```python
import functools

import jax
import jax.numpy as jnp
from jax import lax
from jax.experimental import pallas as pl
from jax.experimental.pallas import tpu as pltpu
from jax.sharding import PartitionSpec as P

AXES = ("label", "sub")
N = 4
STRIDE = {"y": 32, "x": 8, "z": 2}
LANES = 128
SUB = 1024
WSUB = 512
FSUB = 256
VMEM = pltpu.VMEM
WHOLE = pl.BlockSpec(memory_space=VMEM)
SCALARS = pl.BlockSpec(memory_space=pltpu.SMEM)
ORDER = pl.BlockSpec(memory_space=pl.ANY)
STAYS = pl.BlockSpec(memory_space=pltpu.HBM)


def vmem(x):
    return pltpu.with_memory_space_constraint(x, VMEM)


def hbm(x):
    return pltpu.with_memory_space_constraint(x, pltpu.HBM)


def params(mebibytes):
    return pltpu.CompilerParams(vmem_limit_bytes=mebibytes << 20)


def cost(flops):
    return pl.CostEstimate(flops=flops // 8, bytes_accessed=0, transcendentals=0)


STAGES = {"first": ("z", "z"), "second": ("y", "x"), "third": ("x", "y")}


def along(stage, core, chip):
    place = {axis: chip // (step // 2) % N for axis, step in STRIDE.items()}
    axes = STAGES[stage]
    return jnp.where(core == 0, place[axes[0]], place[axes[1]])


def partners(stage, k):
    pairs = []
    for d in range(2 * N * N * N):
        step = STRIDE[STAGES[stage][d % 2]]
        at = d // step % N
        pairs.append((d, d + ((at ^ k) - at) * step))
    return pairs


def exchange(x, stage, k):
    return lax.ppermute(x, AXES, partners(stage, k))


def shifted(stage, k):
    pairs = []
    for d in range(2 * N * N * N):
        step = STRIDE[STAGES[stage][d % 2]]
        at = d // step % N
        pairs.append((d, d + ((at + k) % N - at) * step))
    return pairs


def fetch(x, stage, k):
    return lax.ppermute(x, AXES, shifted(stage, -k))


def push(x, stage, k):
    return lax.ppermute(x, AXES, shifted(stage, k))


def swap(x):
    return lax.ppermute(x, AXES, [(d, d ^ 1) for d in range(2 * N * N * N)])


def prepare_kernel(piece, pos_ref, b1_ref, w_ref, ids_hbm, counts_hbm, b0_hbm, *refs):
    w_out, words_out, half_out, ids_ref, counts_ref, b0_ref, sems = refs[-7:]
    pairs = ((ids_hbm, ids_ref), (counts_hbm, counts_ref), (b0_hbm, b0_ref), (w_ref, w_out))
    copies = [pltpu.make_async_copy(src, dst, sems.at[i]) for i, (src, dst) in enumerate(pairs)]
    for copy in copies:
        copy.start()
    copies[0].wait()
    copies[1].wait()
    core, base, own = pos_ref[0], pos_ref[1], pos_ref[2]
    slots, queries = ids_ref.shape
    row = lax.broadcasted_iota(jnp.int32, (8, LANES), 0)
    slot = lax.broadcasted_iota(jnp.int32, (slots, LANES), 0)
    first, second, third = pos_ref[3], pos_ref[4], pos_ref[5]
    lane = lax.broadcasted_iota(jnp.int32, (slots, LANES), 1)
    kept = (lane // piece) % 2 == core
    shift = jnp.where(core == 0, piece, LANES - piece)

    def packed(ref, q):
        other = pltpu.roll(jnp.broadcast_to(ref[:, q + LANES : q + 2 * LANES], (slots, LANES)), shift, 1)
        return jnp.where(kept, jnp.broadcast_to(ref[:, q : q + LANES], (slots, LANES)), other)

    for q in range(0, queries, 2 * LANES):
        rel = packed(ids_ref, q) - base
        valid = jnp.logical_and(rel >= 0, rel < 2 * own)
        valid = jnp.logical_and(valid, slot < packed(counts_ref, q))
        rel = jnp.where(valid, rel, 0) ^ (core * own)
        bit = jnp.where(valid, lax.shift_left(jnp.ones_like(rel), rel >> 7), 0)
        low = rel & (LANES - 1)
        parts = []
        for g in range(0, LANES, 8):
            word = jnp.zeros((8, LANES), jnp.int32)
            for j in range(slots):
                word = word | jnp.where(low[j : j + 1, :] == row + g, bit[j : j + 1, :], 0)
            parts.append(word)
        words = jnp.concatenate(parts, axis=0).T
        for place in range(LANES // piece):
            near = place % 2 == core
            chip = q // (2 * piece) + place // 2 + jnp.where(near, 0, N)
            at1, at2, at3 = (along(stage, core, chip) for stage in STAGES)
            at1, at2, at3 = (at1 - first + N) % N, (at2 - second + N) % N, at3 ^ third
            row_at = ((at3 * N + at2) * N + at1) * piece
            words_out[pl.ds(pl.multiple_of(row_at, piece), piece), :] = words[place * piece : (place + 1) * piece, :]
    copies[2].wait()
    half_out[...] = 0.5 * jnp.concatenate([b0_ref[...], b1_ref[...]], axis=1)
    copies[3].wait()


def prepare(piece, pos, w, ids, counts, b0, b1, after=()):
    return pl.pallas_call(
        functools.partial(prepare_kernel, piece),
        in_specs=[SCALARS, WHOLE] + [STAYS] * 4 + [ORDER] * len(after),
        out_specs=[WHOLE] * 3,
        out_shape=[
            VMEM(w.shape, w.dtype),
            VMEM((ids.shape[1] // 2, LANES), jnp.int32),
            VMEM((1, 2 * b0.shape[1]), jnp.float32),
        ],
        scratch_shapes=[
            VMEM(ids.shape, ids.dtype),
            VMEM(counts.shape, counts.dtype),
            VMEM(b0.shape, b0.dtype),
            pltpu.SemaphoreType.DMA((4,)),
        ],
        name="prepare",
        cost_estimate=cost(0),
        compiler_params=params(8),
    )(pos, b1, *[hbm(x) for x in (w, ids, counts, b0)], *after)


def load_kernel(x_ref, *refs):
    refs[-1][...] = x_ref[...]


def load(x, after):
    return pl.pallas_call(
        load_kernel,
        in_specs=[WHOLE] + [ORDER] * len(after),
        out_specs=WHOLE,
        out_shape=VMEM(x.shape, x.dtype),
        name="load",
        cost_estimate=cost(0),
        compiler_params=params(4),
    )(hbm(x), *after)


def join_kernel(count, factor, *refs):
    refs[-1][...] = jnp.concatenate([ref[...] for ref in refs[:count]], axis=0) * jnp.bfloat16(factor)


def join(parts, factor=1.0, after=()):
    rows, width = parts[0].shape
    return pl.pallas_call(
        functools.partial(join_kernel, len(parts), factor),
        in_specs=[WHOLE] * len(parts) + [ORDER] * len(after),
        out_specs=WHOLE,
        out_shape=VMEM((len(parts) * rows, width), parts[0].dtype),
        name="join",
        cost_estimate=cost(0),
        compiler_params=params(4),
    )(*[vmem(x) for x in parts], *after)


def residual_kernel(chunk, again, f_ref, w0_ref, w1_ref, b_ref, words_ref, *refs):
    r_ref, o_ref = refs[-3:-1] if again else refs[-2:]
    f = f_ref[...]
    if again:
        refs[-1][...] = f
    rows, own = f.shape[0], w0_ref.shape[0]
    words = words_ref[chunk * rows : (chunk + 1) * rows, :]
    for half, w_ref in enumerate((w0_ref, w1_ref)):
        for s in range(0, own, SUB):
            logits = lax.dot_general(
                f, w_ref[s : s + SUB, :], (((1,), (1,)), ((), ())), preferred_element_type=jnp.float32
            )
            for g in range(0, SUB, LANES):
                at = half * own + s + g
                half_logits = logits[:, g : g + LANES] + b_ref[:, at : at + LANES]
                mark = jnp.int32(1 << (at // LANES) if at // LANES < 31 else -(1 << 31))
                offset = jnp.where((words & mark) != 0, -1.0, 1.0)
                r_ref[:, at : at + LANES] = (jnp.tanh(half_logits) + offset).astype(jnp.bfloat16)
    w = jnp.concatenate([w0_ref[...], w1_ref[...]], axis=0)
    total = jnp.dot(r_ref[...], w, preferred_element_type=jnp.float32)
    o_ref[...] = (total * 0.5).astype(o_ref.dtype)


def residual(chunk, f, w0, w1, b, words, out_type, after=(), again=False):
    rows, width = f.shape
    labels = 2 * w0.shape[0]
    return pl.pallas_call(
        functools.partial(residual_kernel, chunk, again),
        in_specs=[WHOLE] * 5 + [ORDER] * len(after),
        out_specs=[WHOLE] * (3 if again else 2),
        out_shape=[VMEM((rows, labels), jnp.bfloat16), VMEM((rows, width), out_type)] + [VMEM(f.shape, f.dtype)] * again,
        name="residual",
        cost_estimate=cost(4 * rows * labels),
        compiler_params=params(12),
    )(*[vmem(x) for x in (f, w0, w1, b, words)], *after)


def weight_partial_kernel(start, *refs):
    r_refs, f_refs, out_ref = refs[:N], refs[N : 2 * N], refs[-1]
    f = jnp.concatenate([ref[...] for ref in f_refs], axis=0)
    for s in range(0, out_ref.shape[0], WSUB):
        r = jnp.concatenate([ref[:, start + s : start + s + WSUB] for ref in r_refs], axis=0)
        total = lax.dot_general(r, f, (((0,), (0,)), ((), ())), preferred_element_type=jnp.float32)
        out_ref[s : s + WSUB, :] = total.astype(out_ref.dtype)


def weight_partial(rs, fs, start, count, kind, after=()):
    rows, width = fs[0].shape
    return pl.pallas_call(
        functools.partial(weight_partial_kernel, start),
        in_specs=[WHOLE] * (2 * N) + [ORDER] * len(after),
        out_specs=WHOLE,
        out_shape=VMEM((count, width), kind),
        name="weight_partial",
        cost_estimate=cost(2 * rows * count),
        compiler_params=params(12),
    )(*[vmem(x) for x in rs], *[vmem(x) for x in fs], *after)


def weight_rows_kernel(start, *refs):
    r_refs, f_refs, other_ref = refs[:N], refs[N : 2 * N], refs[2 * N]
    out_ref, done_ref, rows_ref, sems = refs[-4:]
    f = jnp.concatenate([ref[...] for ref in f_refs], axis=0)
    copies = []
    for s in range(0, rows_ref.shape[0], WSUB):
        r = jnp.concatenate([ref[:, start + s : start + s + WSUB] for ref in r_refs], axis=0)
        total = lax.dot_general(r, f, (((0,), (0,)), ((), ())), preferred_element_type=jnp.float32)
        total = total + other_ref[s : s + WSUB, :].astype(jnp.float32)
        rows_ref[s : s + WSUB, :] = total.astype(jnp.bfloat16)
        copy = pltpu.make_async_copy(
            rows_ref.at[pl.ds(s, WSUB)], out_ref.at[pl.ds(start + s, WSUB)], sems.at[s // WSUB]
        )
        copy.start()
        copies.append(copy)
    done_ref[...] = jnp.zeros_like(done_ref)
    for copy in copies:
        copy.wait()


def weight_rows(rs, fs, start, count, own, other, after):
    rows, width = fs[0].shape
    return pl.pallas_call(
        functools.partial(weight_rows_kernel, start),
        in_specs=[WHOLE] * (2 * N + 1) + [ORDER] * len(after),
        out_specs=[ORDER, WHOLE],
        out_shape=[jax.ShapeDtypeStruct((own, width), jnp.bfloat16), VMEM((8, LANES), jnp.float32)],
        scratch_shapes=[VMEM((count, width), jnp.bfloat16), pltpu.SemaphoreType.DMA((count // WSUB,))],
        name="weight_rows",
        cost_estimate=cost(16 * N * rows * count * width),
        compiler_params=params(12),
    )(*[vmem(x) for x in rs], *[vmem(x) for x in fs], vmem(other), *after)


def finish_kernel(start, mine_ref, other_ref, *refs):
    out_ref, done_ref, rows_ref, sems = refs[-4:]
    done_ref[...] = jnp.zeros_like(done_ref)
    copies = []
    for i, s in enumerate(range(0, rows_ref.shape[0], FSUB)):
        total = mine_ref[s : s + FSUB, :] + other_ref[s : s + FSUB, :].astype(jnp.float32)
        rows_ref[s : s + FSUB, :] = total.astype(jnp.bfloat16)
        copies.append(
            pltpu.make_async_copy(rows_ref.at[pl.ds(s, FSUB)], out_ref.at[pl.ds(start + s, FSUB)], sems.at[i])
        )
        copies[-1].start()
    for copy in copies:
        copy.wait()


def finish_rows(mine, other, whole, start, after):
    count, width = mine.shape
    return pl.pallas_call(
        functools.partial(finish_kernel, start),
        in_specs=[WHOLE] * 2 + [ORDER] * (1 + len(after)),
        out_specs=[ORDER, WHOLE],
        out_shape=[jax.ShapeDtypeStruct(whole.shape, whole.dtype), VMEM((8, LANES), jnp.float32)],
        scratch_shapes=[VMEM((count, width), jnp.bfloat16), pltpu.SemaphoreType.DMA((count // FSUB,))],
        input_output_aliases={2: 0},
        name="finish_rows",
        cost_estimate=cost(16 * N * count * count * width // 4),
        compiler_params=params(8),
    )(vmem(mine), vmem(other), whole, *after)


def add_kernel(count, own_ref, a_ref, b_ref, c_ref, *refs):
    rows = a_ref.shape[0]
    total = own_ref[:rows, :] + a_ref[...].astype(jnp.float32)
    total = total + b_ref[...].astype(jnp.float32) + c_ref[...].astype(jnp.float32)
    outs = refs[len(refs) - count :]
    step = rows // count
    outs[0][...] = total[:step, :]
    for k in range(1, count):
        outs[k][...] = total[k * step : (k + 1) * step, :].astype(jnp.bfloat16)


def add(own, parts, count, after=()):
    rows, width = parts[0].shape
    kinds = [jnp.float32] + [jnp.bfloat16] * (count - 1)
    return pl.pallas_call(
        functools.partial(add_kernel, count),
        in_specs=[WHOLE] * 4 + [ORDER] * len(after),
        out_specs=[WHOLE] * count,
        out_shape=[(VMEM if count > 1 else jax.ShapeDtypeStruct)((rows // count, width), kind) for kind in kinds],
        name="add",
        cost_estimate=cost(3 * 10**11),
        compiler_params=params(4),
    )(vmem(own), *[vmem(x) for x in parts], *after)


def on_device(features, label_weight, label_bias, positive_ids, positive_counts):
    own, width = label_weight.shape
    piece = features.shape[0]
    me = lax.axis_index(AXES)
    core, chip = me % 2, me // 2
    pos = jnp.stack([core, chip * 2 * own, own] + [along(stage, core, chip) for stage in STAGES])

    b0 = label_bias.reshape(1, own)
    b1 = swap(b0)
    near = [fetch(features, "first", k) for k in (1, 2, 3)]
    f64 = join([load(features, (b1,))] + near, factor=0.5)
    late, f64 = lax.optimization_barrier((label_weight, f64))
    w1 = swap(late)
    w0, words, b = prepare(piece, pos, label_weight, positive_ids.T, positive_counts.reshape(1, -1), b0, b1, after=(f64,))
    f256 = join([f64] + [fetch(f64, "second", k) for k in (1, 2, 3)], after=(words,))
    fs = [f256, exchange(f256, "third", 1), None, exchange(f256, "third", 3)]

    rs = [None] * N
    rs[0], sums, again = residual(0, f256, w0, w1, b, words, jnp.float32, again=True)
    fs[2] = exchange(again, "third", 2)
    arrived, after = [], (sums,)
    for k in (1, 3, 2):
        rs[k], part = residual(k, fs[k], w0, w1, b, words, jnp.bfloat16, after)
        after = (part,)
        arrived.append(exchange(part, "third", k))

    half = own // 2
    partial = functools.partial(weight_partial, rs, fs)
    theirs = [partial(own, half, jnp.bfloat16, arrived[:1]), partial(own + half, half, jnp.bfloat16, arrived[1:2])]
    mine = partial(half, half, jnp.float32, theirs)
    theirs = [swap(x) for x in theirs]
    sums, *sent = add(sums, arrived, N, after=(mine,))
    arrived = [push(x, "second", k) for k, x in zip((1, 2, 3), sent)]
    weight_grad, done = weight_rows(rs, fs, 0, half, own, theirs[0], sent)
    sums, *sent = add(sums, arrived, N, after=(done,))
    arrived = [push(x, "first", k) for k, x in zip((1, 2, 3), sent)]
    weight_grad, done = finish_rows(mine, theirs[1], weight_grad, half, sent)
    (sums,) = add(sums, arrived, 1, after=(done,))
    return weight_grad, sums


def solution(mesh):
    split = P(AXES, None)
    return jax.shard_map(
        on_device,
        mesh=mesh,
        in_specs=(split, split, P(AXES), P(), P()),
        out_specs=(split, split),
        check_vma=False,
    )
```

```python
import functools

import jax
import jax.numpy as jnp
from jax import lax
from jax.experimental import pallas as pl
from jax.experimental.pallas import tpu as pltpu
from jax.sharding import PartitionSpec as P

AXES = ("label", "sub")
N = 4
STRIDE = {"y": 32, "x": 8, "z": 2}
LANES = 128
SUB = 1024
WSUB = 512
FSUB = 256
VMEM = pltpu.VMEM
WHOLE = pl.BlockSpec(memory_space=VMEM)
SCALARS = pl.BlockSpec(memory_space=pltpu.SMEM)
ORDER = pl.BlockSpec(memory_space=pl.ANY)
STAYS = pl.BlockSpec(memory_space=pltpu.HBM)


def vmem(x):
    return pltpu.with_memory_space_constraint(x, VMEM)


def hbm(x):
    return pltpu.with_memory_space_constraint(x, pltpu.HBM)


def params(mebibytes):
    return pltpu.CompilerParams(vmem_limit_bytes=mebibytes << 20)


def cost(flops):
    return pl.CostEstimate(flops=flops // 8, bytes_accessed=0, transcendentals=0)


STAGES = {"first": ("z", "z"), "second": ("y", "x"), "third": ("x", "y")}


def along(stage, core, chip):
    place = {axis: chip // (step // 2) % N for axis, step in STRIDE.items()}
    axes = STAGES[stage]
    return jnp.where(core == 0, place[axes[0]], place[axes[1]])


def partners(stage, k):
    pairs = []
    for d in range(2 * N * N * N):
        step = STRIDE[STAGES[stage][d % 2]]
        at = d // step % N
        pairs.append((d, d + ((at ^ k) - at) * step))
    return pairs


def exchange(x, stage, k):
    return lax.ppermute(x, AXES, partners(stage, k))


def shifted(stage, k):
    pairs = []
    for d in range(2 * N * N * N):
        step = STRIDE[STAGES[stage][d % 2]]
        at = d // step % N
        pairs.append((d, d + ((at + k) % N - at) * step))
    return pairs


def fetch(x, stage, k):
    return lax.ppermute(x, AXES, shifted(stage, -k))


def push(x, stage, k):
    return lax.ppermute(x, AXES, shifted(stage, k))


ORDERED = (0, 2, 1, 3)


def swap(x):
    return lax.ppermute(x, AXES, [(d, d ^ 1) for d in range(2 * N * N * N)])


def prepare_kernel(piece, pos_ref, b1_ref, w_ref, ids_hbm, counts_hbm, b0_hbm, *refs):
    w_out, words_out, half_out, ids_ref, counts_ref, b0_ref, sems = refs[-7:]
    pairs = ((ids_hbm, ids_ref), (counts_hbm, counts_ref), (b0_hbm, b0_ref), (w_ref, w_out))
    copies = [pltpu.make_async_copy(src, dst, sems.at[i]) for i, (src, dst) in enumerate(pairs)]
    for copy in copies:
        copy.start()
    copies[0].wait()
    copies[1].wait()
    core, base, own = pos_ref[0], pos_ref[1], pos_ref[2]
    slots, queries = ids_ref.shape
    row = lax.broadcasted_iota(jnp.int32, (8, LANES), 0)
    slot = lax.broadcasted_iota(jnp.int32, (slots, LANES), 0)
    first, second, third = pos_ref[3], pos_ref[4], pos_ref[5]
    lane = lax.broadcasted_iota(jnp.int32, (slots, LANES), 1)
    kept = (lane // piece) % 2 == core
    shift = jnp.where(core == 0, piece, LANES - piece)

    def packed(ref, q):
        other = pltpu.roll(jnp.broadcast_to(ref[:, q + LANES : q + 2 * LANES], (slots, LANES)), shift, 1)
        return jnp.where(kept, jnp.broadcast_to(ref[:, q : q + LANES], (slots, LANES)), other)

    for q in range(0, queries, 2 * LANES):
        rel = packed(ids_ref, q) - base
        valid = jnp.logical_and(rel >= 0, rel < 2 * own)
        valid = jnp.logical_and(valid, slot < packed(counts_ref, q))
        rel = jnp.where(valid, rel, 0) ^ (core * own)
        bit = jnp.where(valid, lax.shift_left(jnp.ones_like(rel), rel >> 7), 0)
        low = rel & (LANES - 1)
        parts = []
        for g in range(0, LANES, 8):
            word = jnp.zeros((8, LANES), jnp.int32)
            for j in range(slots):
                word = word | jnp.where(low[j : j + 1, :] == row + g, bit[j : j + 1, :], 0)
            parts.append(word)
        words = jnp.concatenate(parts, axis=0).T
        for place in range(LANES // piece):
            near = place % 2 == core
            chip = q // (2 * piece) + place // 2 + jnp.where(near, 0, N)
            at1, at2, at3 = (along(stage, core, chip) for stage in STAGES)
            at1, at2, at3 = (at1 - first + N) % N, (at2 - second + N) % N, at3 ^ third
            row_at = ((at3 * N + at2) * N + at1) * piece
            words_out[pl.ds(pl.multiple_of(row_at, piece), piece), :] = words[place * piece : (place + 1) * piece, :]
    copies[2].wait()
    half_out[...] = 0.5 * jnp.concatenate([b0_ref[...], b1_ref[...]], axis=1)
    copies[3].wait()


def prepare(piece, pos, w, ids, counts, b0, b1, after=()):
    return pl.pallas_call(
        functools.partial(prepare_kernel, piece),
        in_specs=[SCALARS, WHOLE] + [STAYS] * 4 + [ORDER] * len(after),
        out_specs=[WHOLE] * 3,
        out_shape=[
            VMEM(w.shape, w.dtype),
            VMEM((ids.shape[1] // 2, LANES), jnp.int32),
            VMEM((1, 2 * b0.shape[1]), jnp.float32),
        ],
        scratch_shapes=[
            VMEM(ids.shape, ids.dtype),
            VMEM(counts.shape, counts.dtype),
            VMEM(b0.shape, b0.dtype),
            pltpu.SemaphoreType.DMA((4,)),
        ],
        name="prepare",
        cost_estimate=cost(0),
        compiler_params=params(8),
    )(pos, b1, *[hbm(x) for x in (w, ids, counts, b0)], *after)


def load_kernel(x_ref, *refs):
    refs[-1][...] = x_ref[...]


def load(x, after):
    return pl.pallas_call(
        load_kernel,
        in_specs=[WHOLE] + [ORDER] * len(after),
        out_specs=WHOLE,
        out_shape=VMEM(x.shape, x.dtype),
        name="load",
        cost_estimate=cost(0),
        compiler_params=params(4),
    )(hbm(x), *after)


def join_kernel(count, factor, *refs):
    refs = [refs[ORDERED.index(k)] for k in range(count)] + [refs[-1]]
    refs[-1][...] = jnp.concatenate([ref[...] for ref in refs[:count]], axis=0) * jnp.bfloat16(factor)


def join(parts, factor=1.0, after=()):
    rows, width = parts[0].shape
    return pl.pallas_call(
        functools.partial(join_kernel, len(parts), factor),
        in_specs=[WHOLE] * len(parts) + [ORDER] * len(after),
        out_specs=WHOLE,
        out_shape=VMEM((len(parts) * rows, width), parts[0].dtype),
        name="join",
        cost_estimate=cost(0),
        compiler_params=params(4),
    )(*[vmem(x) for x in parts], *after)


def residual_kernel(chunk, again, f_ref, w0_ref, w1_ref, b_ref, words_ref, *refs):
    r_ref, o_ref = refs[-3:-1] if again else refs[-2:]
    f = f_ref[...]
    if again:
        refs[-1][...] = f
    rows, own = f.shape[0], w0_ref.shape[0]
    words = words_ref[chunk * rows : (chunk + 1) * rows, :]
    for half, w_ref in enumerate((w0_ref, w1_ref)):
        for s in range(0, own, SUB):
            logits = lax.dot_general(
                f, w_ref[s : s + SUB, :], (((1,), (1,)), ((), ())), preferred_element_type=jnp.float32
            )
            for g in range(0, SUB, LANES):
                at = half * own + s + g
                half_logits = logits[:, g : g + LANES] + b_ref[:, at : at + LANES]
                mark = jnp.int32(1 << (at // LANES) if at // LANES < 31 else -(1 << 31))
                offset = jnp.where((words & mark) != 0, -1.0, 1.0)
                r_ref[:, at : at + LANES] = (jnp.tanh(half_logits) + offset).astype(jnp.bfloat16)
    w = jnp.concatenate([w0_ref[...], w1_ref[...]], axis=0)
    total = jnp.dot(r_ref[...], w, preferred_element_type=jnp.float32)
    o_ref[...] = (total * 0.5).astype(o_ref.dtype)


def residual(chunk, f, w0, w1, b, words, out_type, after=(), again=False):
    rows, width = f.shape
    labels = 2 * w0.shape[0]
    return pl.pallas_call(
        functools.partial(residual_kernel, chunk, again),
        in_specs=[WHOLE] * 5 + [ORDER] * len(after),
        out_specs=[WHOLE] * (3 if again else 2),
        out_shape=[VMEM((rows, labels), jnp.bfloat16), VMEM((rows, width), out_type)] + [VMEM(f.shape, f.dtype)] * again,
        name="residual",
        cost_estimate=cost(4 * rows * labels),
        compiler_params=params(12),
    )(*[vmem(x) for x in (f, w0, w1, b, words)], *after)


def weight_partial_kernel(start, *refs):
    r_refs, f_refs, out_ref = refs[:N], refs[N : 2 * N], refs[-1]
    f = jnp.concatenate([ref[...] for ref in f_refs], axis=0)
    for s in range(0, out_ref.shape[0], WSUB):
        r = jnp.concatenate([ref[:, start + s : start + s + WSUB] for ref in r_refs], axis=0)
        total = lax.dot_general(r, f, (((0,), (0,)), ((), ())), preferred_element_type=jnp.float32)
        out_ref[s : s + WSUB, :] = total.astype(out_ref.dtype)


def weight_partial(rs, fs, start, count, kind, after=()):
    rows, width = fs[0].shape
    return pl.pallas_call(
        functools.partial(weight_partial_kernel, start),
        in_specs=[WHOLE] * (2 * N) + [ORDER] * len(after),
        out_specs=WHOLE,
        out_shape=VMEM((count, width), kind),
        name="weight_partial",
        cost_estimate=cost(2 * rows * count),
        compiler_params=params(12),
    )(*[vmem(x) for x in rs], *[vmem(x) for x in fs], *after)


def weight_rows_kernel(start, *refs):
    r_refs, f_refs, other_ref = refs[:N], refs[N : 2 * N], refs[2 * N]
    out_ref, done_ref, rows_ref, sems = refs[-4:]
    f = jnp.concatenate([ref[...] for ref in f_refs], axis=0)
    copies = []
    for s in range(0, rows_ref.shape[0], WSUB):
        r = jnp.concatenate([ref[:, start + s : start + s + WSUB] for ref in r_refs], axis=0)
        total = lax.dot_general(r, f, (((0,), (0,)), ((), ())), preferred_element_type=jnp.float32)
        total = total + other_ref[s : s + WSUB, :].astype(jnp.float32)
        rows_ref[s : s + WSUB, :] = total.astype(jnp.bfloat16)
        copy = pltpu.make_async_copy(
            rows_ref.at[pl.ds(s, WSUB)], out_ref.at[pl.ds(start + s, WSUB)], sems.at[s // WSUB]
        )
        copy.start()
        copies.append(copy)
    done_ref[...] = jnp.zeros_like(done_ref)
    for copy in copies:
        copy.wait()


def weight_rows(rs, fs, start, count, own, other, after):
    rows, width = fs[0].shape
    return pl.pallas_call(
        functools.partial(weight_rows_kernel, start),
        in_specs=[WHOLE] * (2 * N + 1) + [ORDER] * len(after),
        out_specs=[ORDER, WHOLE],
        out_shape=[jax.ShapeDtypeStruct((own, width), jnp.bfloat16), VMEM((8, LANES), jnp.float32)],
        scratch_shapes=[VMEM((count, width), jnp.bfloat16), pltpu.SemaphoreType.DMA((count // WSUB,))],
        name="weight_rows",
        cost_estimate=cost(16 * N * rows * count * width),
        compiler_params=params(12),
    )(*[vmem(x) for x in rs], *[vmem(x) for x in fs], vmem(other), *after)


def finish_kernel(start, mine_ref, other_ref, *refs):
    out_ref, done_ref, rows_ref, sems = refs[-4:]
    done_ref[...] = jnp.zeros_like(done_ref)
    copies = []
    for i, s in enumerate(range(0, rows_ref.shape[0], FSUB)):
        total = mine_ref[s : s + FSUB, :] + other_ref[s : s + FSUB, :].astype(jnp.float32)
        rows_ref[s : s + FSUB, :] = total.astype(jnp.bfloat16)
        copies.append(
            pltpu.make_async_copy(rows_ref.at[pl.ds(s, FSUB)], out_ref.at[pl.ds(start + s, FSUB)], sems.at[i])
        )
        copies[-1].start()
    for copy in copies:
        copy.wait()


def finish_rows(mine, other, whole, start, after):
    count, width = mine.shape
    return pl.pallas_call(
        functools.partial(finish_kernel, start),
        in_specs=[WHOLE] * 2 + [ORDER] * (1 + len(after)),
        out_specs=[ORDER, WHOLE],
        out_shape=[jax.ShapeDtypeStruct(whole.shape, whole.dtype), VMEM((8, LANES), jnp.float32)],
        scratch_shapes=[VMEM((count, width), jnp.bfloat16), pltpu.SemaphoreType.DMA((count // FSUB,))],
        input_output_aliases={2: 0},
        name="finish_rows",
        cost_estimate=cost(16 * N * count * count * width // 4),
        compiler_params=params(8),
    )(vmem(mine), vmem(other), whole, *after)


def add_kernel(count, own_ref, a_ref, b_ref, c_ref, *refs):
    rows = a_ref.shape[0]
    total = own_ref[:rows, :] + a_ref[...].astype(jnp.float32)
    total = total + b_ref[...].astype(jnp.float32) + c_ref[...].astype(jnp.float32)
    outs = refs[len(refs) - count :]
    step = rows // count
    outs[0][...] = total[:step, :]
    for k in range(1, count):
        outs[k][...] = total[k * step : (k + 1) * step, :].astype(jnp.bfloat16)


def add(own, parts, count, after=()):
    rows, width = parts[0].shape
    kinds = [jnp.float32] + [jnp.bfloat16] * (count - 1)
    return pl.pallas_call(
        functools.partial(add_kernel, count),
        in_specs=[WHOLE] * 4 + [ORDER] * len(after),
        out_specs=[WHOLE] * count,
        out_shape=[(VMEM if count > 1 else jax.ShapeDtypeStruct)((rows // count, width), kind) for kind in kinds],
        name="add",
        cost_estimate=cost(3 * 10**11),
        compiler_params=params(4),
    )(vmem(own), *[vmem(x) for x in parts], *after)


def on_device(features, label_weight, label_bias, positive_ids, positive_counts):
    own, width = label_weight.shape
    piece = features.shape[0]
    me = lax.axis_index(AXES)
    core, chip = me % 2, me // 2
    pos = jnp.stack([core, chip * 2 * own, own] + [along(stage, core, chip) for stage in STAGES])

    b0 = label_bias.reshape(1, own)
    b1 = swap(b0)
    near = [fetch(features, "first", k) for k in ORDERED[1:]]
    f64 = join([load(features, (b1,))] + near, factor=0.5)
    late, f64 = lax.optimization_barrier((label_weight, f64))
    w1 = swap(late)
    w0, words, b = prepare(piece, pos, label_weight, positive_ids.T, positive_counts.reshape(1, -1), b0, b1, after=(f64,))
    f256 = join([f64] + [fetch(f64, "second", k) for k in ORDERED[1:]], after=(words,))
    fs = [f256, exchange(f256, "third", 1), None, exchange(f256, "third", 3)]

    rs = [None] * N
    rs[0], sums, again = residual(0, f256, w0, w1, b, words, jnp.float32, again=True)
    fs[2] = exchange(again, "third", 2)
    arrived, after = [], (sums,)
    for k in (1, 3, 2):
        rs[k], part = residual(k, fs[k], w0, w1, b, words, jnp.bfloat16, after)
        after = (part,)
        arrived.append(exchange(part, "third", k))

    half = own // 2
    partial = functools.partial(weight_partial, rs, fs)
    theirs = [partial(own, half, jnp.bfloat16, arrived[:1]), partial(own + half, half, jnp.bfloat16, arrived[1:2])]
    mine = partial(half, half, jnp.float32, theirs)
    theirs = [swap(x) for x in theirs]
    sums, *sent = add(sums, arrived, N, after=(mine,))
    arrived = [push(sent[k - 1], "second", k) for k in ORDERED[1:]]
    weight_grad, done = weight_rows(rs, fs, 0, half, own, theirs[0], sent)
    sums, *sent = add(sums, arrived, N, after=(done,))
    arrived = [push(sent[k - 1], "first", k) for k in ORDERED[1:]]
    weight_grad, done = finish_rows(mine, theirs[1], weight_grad, half, sent)
    (sums,) = add(sums, arrived, 1, after=(done,))
    return weight_grad, sums


def solution(mesh):
    split = P(AXES, None)
    return jax.shard_map(
        on_device,
        mesh=mesh,
        in_specs=(split, split, P(AXES), P(), P()),
        out_specs=(split, split),
        check_vma=False,
    )
```

```python
import functools

import jax
import jax.numpy as jnp
from jax import lax
from jax.experimental import pallas as pl
from jax.experimental.pallas import tpu as pltpu
from jax.sharding import PartitionSpec as P

AXES = ("label", "sub")
N = 4
STRIDE = {"y": 32, "x": 8, "z": 2}
LANES = 128
SUB = 1024
WSUB = 512
FSUB = 256
VMEM = pltpu.VMEM
WHOLE = pl.BlockSpec(memory_space=VMEM)
SCALARS = pl.BlockSpec(memory_space=pltpu.SMEM)
ORDER = pl.BlockSpec(memory_space=pl.ANY)
STAYS = pl.BlockSpec(memory_space=pltpu.HBM)


def vmem(x):
    return pltpu.with_memory_space_constraint(x, VMEM)


def hbm(x):
    return pltpu.with_memory_space_constraint(x, pltpu.HBM)


def params(mebibytes):
    return pltpu.CompilerParams(vmem_limit_bytes=mebibytes << 20)


def cost(flops):
    return pl.CostEstimate(flops=flops // 8, bytes_accessed=0, transcendentals=0)


STAGES = {"first": ("z", "z"), "second": ("y", "x"), "third": ("x", "y")}


def along(stage, core, chip):
    place = {axis: chip // (step // 2) % N for axis, step in STRIDE.items()}
    axes = STAGES[stage]
    return jnp.where(core == 0, place[axes[0]], place[axes[1]])


def partners(stage, k):
    pairs = []
    for d in range(2 * N * N * N):
        step = STRIDE[STAGES[stage][d % 2]]
        at = d // step % N
        pairs.append((d, d + ((at ^ k) - at) * step))
    return pairs


def exchange(x, stage, k):
    return lax.ppermute(x, AXES, partners(stage, k))


def shifted(stage, k):
    pairs = []
    for d in range(2 * N * N * N):
        step = STRIDE[STAGES[stage][d % 2]]
        at = d // step % N
        pairs.append((d, d + ((at + k) % N - at) * step))
    return pairs


def fetch(x, stage, k):
    return lax.ppermute(x, AXES, shifted(stage, -k))


def push(x, stage, k):
    return lax.ppermute(x, AXES, shifted(stage, k))


ORDERED = (0, 2, 1, 3)


def swap(x):
    return lax.ppermute(x, AXES, [(d, d ^ 1) for d in range(2 * N * N * N)])


def prepare_kernel(piece, pos_ref, b1_ref, w_ref, ids_hbm, counts_hbm, b0_hbm, *refs):
    w_out, words_out, half_out, ids_ref, counts_ref, b0_ref, sems = refs[-7:]
    pairs = ((ids_hbm, ids_ref), (counts_hbm, counts_ref), (b0_hbm, b0_ref), (w_ref, w_out))
    copies = [pltpu.make_async_copy(src, dst, sems.at[i]) for i, (src, dst) in enumerate(pairs)]
    for copy in copies:
        copy.start()
    copies[0].wait()
    copies[1].wait()
    core, base, own = pos_ref[0], pos_ref[1], pos_ref[2]
    slots, queries = ids_ref.shape
    row = lax.broadcasted_iota(jnp.int32, (8, LANES), 0)
    slot = lax.broadcasted_iota(jnp.int32, (slots, LANES), 0)
    first, second, third = pos_ref[3], pos_ref[4], pos_ref[5]
    lane = lax.broadcasted_iota(jnp.int32, (slots, LANES), 1)
    kept = (lane // piece) % 2 == core
    shift = jnp.where(core == 0, piece, LANES - piece)

    def packed(ref, q):
        other = pltpu.roll(jnp.broadcast_to(ref[:, q + LANES : q + 2 * LANES], (slots, LANES)), shift, 1)
        return jnp.where(kept, jnp.broadcast_to(ref[:, q : q + LANES], (slots, LANES)), other)

    for q in range(0, queries, 2 * LANES):
        rel = packed(ids_ref, q) - base
        valid = jnp.logical_and(rel >= 0, rel < 2 * own)
        valid = jnp.logical_and(valid, slot < packed(counts_ref, q))
        rel = jnp.where(valid, rel, 0) ^ (core * own)
        bit = jnp.where(valid, lax.shift_left(jnp.ones_like(rel), rel >> 7), 0)
        low = rel & (LANES - 1)
        parts = []
        for g in range(0, LANES, 8):
            word = jnp.zeros((8, LANES), jnp.int32)
            for j in range(slots):
                word = word | jnp.where(low[j : j + 1, :] == row + g, bit[j : j + 1, :], 0)
            parts.append(word)
        words = jnp.concatenate(parts, axis=0).T
        for place in range(LANES // piece):
            near = place % 2 == core
            chip = q // (2 * piece) + place // 2 + jnp.where(near, 0, N)
            at1, at2, at3 = (along(stage, core, chip) for stage in STAGES)
            at1, at2, at3 = (at1 - first + N) % N, (at2 - second + N) % N, at3 ^ third
            row_at = ((at3 * N + at2) * N + at1) * piece
            words_out[pl.ds(pl.multiple_of(row_at, piece), piece), :] = words[place * piece : (place + 1) * piece, :]
    copies[2].wait()
    half_out[...] = 0.5 * jnp.concatenate([b0_ref[...], b1_ref[...]], axis=1)
    copies[3].wait()


def prepare(piece, pos, w, ids, counts, b0, b1, after=()):
    return pl.pallas_call(
        functools.partial(prepare_kernel, piece),
        in_specs=[SCALARS, WHOLE] + [STAYS] * 4 + [ORDER] * len(after),
        out_specs=[WHOLE] * 3,
        out_shape=[
            VMEM(w.shape, w.dtype),
            VMEM((ids.shape[1] // 2, LANES), jnp.int32),
            VMEM((1, 2 * b0.shape[1]), jnp.float32),
        ],
        scratch_shapes=[
            VMEM(ids.shape, ids.dtype),
            VMEM(counts.shape, counts.dtype),
            VMEM(b0.shape, b0.dtype),
            pltpu.SemaphoreType.DMA((4,)),
        ],
        name="prepare",
        cost_estimate=cost(0),
        compiler_params=params(8),
    )(pos, b1, *[hbm(x) for x in (w, ids, counts, b0)], *after)


def load_kernel(x_ref, *refs):
    refs[-1][...] = x_ref[...]


def load(x, after):
    return pl.pallas_call(
        load_kernel,
        in_specs=[WHOLE] + [ORDER] * len(after),
        out_specs=WHOLE,
        out_shape=VMEM(x.shape, x.dtype),
        name="load",
        cost_estimate=cost(0),
        compiler_params=params(4),
    )(hbm(x), *after)


def join_kernel(count, factor, *refs):
    refs = [refs[ORDERED.index(k)] for k in range(count)] + [refs[-1]]
    refs[-1][...] = jnp.concatenate([ref[...] for ref in refs[:count]], axis=0) * jnp.bfloat16(factor)


def join(parts, factor=1.0, after=()):
    rows, width = parts[0].shape
    return pl.pallas_call(
        functools.partial(join_kernel, len(parts), factor),
        in_specs=[WHOLE] * len(parts) + [ORDER] * len(after),
        out_specs=WHOLE,
        out_shape=VMEM((len(parts) * rows, width), parts[0].dtype),
        name="join",
        cost_estimate=cost(0),
        compiler_params=params(4),
    )(*[vmem(x) for x in parts], *after)


def residual_kernel(chunk, again, f_ref, w0_ref, w1_ref, b_ref, words_ref, *refs):
    r_ref, o_ref = refs[-3:-1] if again else refs[-2:]
    f = f_ref[...]
    if again:
        refs[-1][...] = f
    rows, own = f.shape[0], w0_ref.shape[0]
    words = words_ref[chunk * rows : (chunk + 1) * rows, :]
    for half, w_ref in enumerate((w0_ref, w1_ref)):
        for s in range(0, own, SUB):
            logits = lax.dot_general(
                f, w_ref[s : s + SUB, :], (((1,), (1,)), ((), ())), preferred_element_type=jnp.float32
            )
            for g in range(0, SUB, LANES):
                at = half * own + s + g
                half_logits = logits[:, g : g + LANES] + b_ref[:, at : at + LANES]
                mark = jnp.int32(1 << (at // LANES) if at // LANES < 31 else -(1 << 31))
                offset = jnp.where((words & mark) != 0, -1.0, 1.0)
                r_ref[:, at : at + LANES] = (jnp.tanh(half_logits) + offset).astype(jnp.bfloat16)
    w = jnp.concatenate([w0_ref[...], w1_ref[...]], axis=0)
    total = jnp.dot(r_ref[...], w, preferred_element_type=jnp.float32)
    o_ref[...] = (total * 0.5).astype(o_ref.dtype)


def residual(chunk, f, w0, w1, b, words, out_type, after=(), again=False):
    rows, width = f.shape
    labels = 2 * w0.shape[0]
    return pl.pallas_call(
        functools.partial(residual_kernel, chunk, again),
        in_specs=[WHOLE] * 5 + [ORDER] * len(after),
        out_specs=[WHOLE] * (3 if again else 2),
        out_shape=[VMEM((rows, labels), jnp.bfloat16), VMEM((rows, width), out_type)] + [VMEM(f.shape, f.dtype)] * again,
        name="residual",
        cost_estimate=cost(4 * rows * labels),
        compiler_params=params(12),
    )(*[vmem(x) for x in (f, w0, w1, b, words)], *after)


def weight_partial_kernel(start, *refs):
    r_refs, f_refs, out_ref = refs[:N], refs[N : 2 * N], refs[-1]
    f = jnp.concatenate([ref[...] for ref in f_refs], axis=0)
    for s in range(0, out_ref.shape[0], WSUB):
        r = jnp.concatenate([ref[:, start + s : start + s + WSUB] for ref in r_refs], axis=0)
        total = lax.dot_general(r, f, (((0,), (0,)), ((), ())), preferred_element_type=jnp.float32)
        out_ref[s : s + WSUB, :] = total.astype(out_ref.dtype)


def weight_partial(rs, fs, start, count, kind, after=()):
    rows, width = fs[0].shape
    return pl.pallas_call(
        functools.partial(weight_partial_kernel, start),
        in_specs=[WHOLE] * (2 * N) + [ORDER] * len(after),
        out_specs=WHOLE,
        out_shape=VMEM((count, width), kind),
        name="weight_partial",
        cost_estimate=cost(2 * rows * count),
        compiler_params=params(12),
    )(*[vmem(x) for x in rs], *[vmem(x) for x in fs], *after)


def weight_rows_kernel(start, *refs):
    r_refs, f_refs, other_ref = refs[:N], refs[N : 2 * N], refs[2 * N]
    out_ref, done_ref, rows_ref, sems = refs[-4:]
    f = jnp.concatenate([ref[...] for ref in f_refs], axis=0)
    copies = []
    for s in range(0, rows_ref.shape[0], WSUB):
        r = jnp.concatenate([ref[:, start + s : start + s + WSUB] for ref in r_refs], axis=0)
        total = lax.dot_general(r, f, (((0,), (0,)), ((), ())), preferred_element_type=jnp.float32)
        total = total + other_ref[s : s + WSUB, :].astype(jnp.float32)
        rows_ref[s : s + WSUB, :] = total.astype(jnp.bfloat16)
        copy = pltpu.make_async_copy(
            rows_ref.at[pl.ds(s, WSUB)], out_ref.at[pl.ds(start + s, WSUB)], sems.at[s // WSUB]
        )
        copy.start()
        copies.append(copy)
    done_ref[...] = jnp.zeros_like(done_ref)
    for copy in copies:
        copy.wait()


def weight_rows(rs, fs, start, count, own, other, after):
    rows, width = fs[0].shape
    return pl.pallas_call(
        functools.partial(weight_rows_kernel, start),
        in_specs=[WHOLE] * (2 * N + 1) + [ORDER] * len(after),
        out_specs=[ORDER, WHOLE],
        out_shape=[jax.ShapeDtypeStruct((own, width), jnp.bfloat16), VMEM((8, LANES), jnp.float32)],
        scratch_shapes=[VMEM((count, width), jnp.bfloat16), pltpu.SemaphoreType.DMA((count // WSUB,))],
        name="weight_rows",
        cost_estimate=cost(16 * N * rows * count * width),
        compiler_params=params(12),
    )(*[vmem(x) for x in rs], *[vmem(x) for x in fs], vmem(other), *after)


def finish_kernel(start, mine_ref, other_ref, *refs):
    out_ref, done_ref, rows_ref, sems = refs[-4:]
    done_ref[...] = jnp.zeros_like(done_ref)
    copies = []
    for i, s in enumerate(range(0, rows_ref.shape[0], FSUB)):
        total = mine_ref[s : s + FSUB, :] + other_ref[s : s + FSUB, :].astype(jnp.float32)
        rows_ref[s : s + FSUB, :] = total.astype(jnp.bfloat16)
        copies.append(
            pltpu.make_async_copy(rows_ref.at[pl.ds(s, FSUB)], out_ref.at[pl.ds(start + s, FSUB)], sems.at[i])
        )
        copies[-1].start()
    for copy in copies:
        copy.wait()


def finish_rows(mine, other, whole, start, after):
    count, width = mine.shape
    return pl.pallas_call(
        functools.partial(finish_kernel, start),
        in_specs=[WHOLE] * 2 + [ORDER] * (1 + len(after)),
        out_specs=[ORDER, WHOLE],
        out_shape=[jax.ShapeDtypeStruct(whole.shape, whole.dtype), VMEM((8, LANES), jnp.float32)],
        scratch_shapes=[VMEM((count, width), jnp.bfloat16), pltpu.SemaphoreType.DMA((count // FSUB,))],
        input_output_aliases={2: 0},
        name="finish_rows",
        cost_estimate=cost(16 * N * count * count * width // 4),
        compiler_params=params(8),
    )(vmem(mine), vmem(other), whole, *after)


def add_kernel(count, own_ref, a_ref, b_ref, c_ref, *refs):
    rows = a_ref.shape[0]
    total = own_ref[:rows, :] + a_ref[...].astype(jnp.float32)
    total = total + b_ref[...].astype(jnp.float32) + c_ref[...].astype(jnp.float32)
    outs = refs[len(refs) - count :]
    step = rows // count
    outs[0][...] = total[:step, :]
    for k in range(1, count):
        outs[k][...] = total[k * step : (k + 1) * step, :].astype(jnp.bfloat16)


def add(own, parts, count, after=()):
    rows, width = parts[0].shape
    kinds = [jnp.float32] + [jnp.bfloat16] * (count - 1)
    return pl.pallas_call(
        functools.partial(add_kernel, count),
        in_specs=[WHOLE] * 4 + [ORDER] * len(after),
        out_specs=[WHOLE] * count,
        out_shape=[(VMEM if count > 1 else jax.ShapeDtypeStruct)((rows // count, width), kind) for kind in kinds],
        name="add",
        cost_estimate=cost(3 * 10**11),
        compiler_params=params(4),
    )(vmem(own), *[vmem(x) for x in parts], *after)


def on_device(features, label_weight, label_bias, positive_ids, positive_counts):
    own, width = label_weight.shape
    piece = features.shape[0]
    me = lax.axis_index(AXES)
    core, chip = me % 2, me // 2
    pos = jnp.stack([core, chip * 2 * own, own] + [along(stage, core, chip) for stage in STAGES])

    b0 = label_bias.reshape(1, own)
    b1 = swap(b0)
    near = [fetch(features, "first", k) for k in ORDERED[1:]]
    f64 = join([load(features, ())] + near, factor=0.5, after=(b1,))
    late, f64 = lax.optimization_barrier((label_weight, f64))
    w1 = swap(late)
    w0, words, b = prepare(piece, pos, label_weight, positive_ids.T, positive_counts.reshape(1, -1), b0, b1, after=(f64,))
    f256 = join([f64] + [fetch(f64, "second", k) for k in ORDERED[1:]], after=(words,))
    fs = [f256, exchange(f256, "third", 1), None, exchange(f256, "third", 3)]

    rs = [None] * N
    rs[0], sums, again = residual(0, f256, w0, w1, b, words, jnp.float32, again=True)
    fs[2] = exchange(again, "third", 2)
    arrived, after = [], (sums,)
    for k in (1, 3, 2):
        rs[k], part = residual(k, fs[k], w0, w1, b, words, jnp.bfloat16, after)
        after = (part,)
        arrived.append(exchange(part, "third", k))

    half = own // 2
    partial = functools.partial(weight_partial, rs, fs)
    theirs = [partial(own, half, jnp.bfloat16, arrived[:1]), partial(own + half, half, jnp.bfloat16, arrived[1:2])]
    mine = partial(half, half, jnp.float32, theirs)
    theirs = [swap(x) for x in theirs]
    sums, *sent = add(sums, arrived, N, after=(mine,))
    arrived = [push(sent[k - 1], "second", k) for k in ORDERED[1:]]
    weight_grad, done = weight_rows(rs, fs, 0, half, own, theirs[0], sent)
    sums, *sent = add(sums, arrived, N, after=(done,))
    arrived = [push(sent[k - 1], "first", k) for k in ORDERED[1:]]
    weight_grad, done = finish_rows(mine, theirs[1], weight_grad, half, sent)
    (sums,) = add(sums, arrived, 1, after=(done,))
    return weight_grad, sums


def solution(mesh):
    split = P(AXES, None)
    return jax.shard_map(
        on_device,
        mesh=mesh,
        in_specs=(split, split, P(AXES), P(), P()),
        out_specs=(split, split),
        check_vma=False,
    )
```
